32 devices in a mesh: ens: 2 (over y), lon: 4 (over z), lat: 4 (over x, core).
Axes of the slice: x: 2, y: 2, z: 4, core: 2. Of those that a mesh axis runs over, the one named last changes fastest.
Arguments:
- state: float32 [32, 512, 512], P('ens', 'lat', 'lon'), parts along dimension 0, may hold values from -6 to 6
- cotangent: float32 [32, 512, 512], P('ens', 'lat', 'lon'), parts along dimension 0, may hold values from -8 to 8
- land_mask: int32 [512, 512], P('lat', 'lon'), may hold values from 0 to 1, as said below
- level_count: int32 [512, 512], P('lat', 'lon'), may hold values from 1 to 16
- fold_partner: int32 [512], P('lon'), may hold values from 0 to 511, as said below
- weight_in: bfloat16 [32, 256], replicated, may hold values from -1 to 1
- weight_out: bfloat16 [256, 16], replicated, may hold values from -0.375 to 0.375
- bias_hidden: float32 [256], replicated, may hold values from -3 to 3
Outputs:
- adjoint_in: float32 [32, 512, 512], P('ens', 'lat', 'lon'), parts along dimension 0
- grad_in: float32 [64, 256], P('ens'), parts along dimension 0
- grad_out: float32 [512, 16], P('ens'), parts along dimension 0
- grad_bias: float32 [512], P('ens'), parts along dimension 0
The draws below stay inside these ranges and needn't reach their ends.
There are 2 independent parts, one for each index of `ens`. The reference program is written for one: setup_inputs(seed, part) draws one part's arguments, and reference() takes and returns one part's arrays. A program takes and returns all parts, laid end to end along the dimension named above; an argument that names none is the same for every part. Nothing has to cross between parts.
Inputs may be any that keep to these rules, and one draw needn't show every extreme that they name: fold_partner[i] = (c - i) modulo 512 for one even whole number c, so fold_partner[fold_partner[i]] = i. `land_mask`: the top two rows are all ocean.
All inputs are finite; a program needn't handle non-finite values.
Results may differ from the reference program's by a relative error of at most 0.0029.
Values sent between devices are 32-bit elements; how exact they have to be, the bound alone decides.
A program may use at most 64 MiB of HBM per device.

```python
import math
import jax
import jax.numpy as jnp
from jax import lax

L = 16
H = 256
ITERS = 3
CLAT = 128
CLON = 128
NLAT = 512
NLON = 512


def draw_fold_partner(key, part):
    key = jax.random.fold_in(key, 7)
    centre = 2 * jax.random.randint(key, (), 0, NLON // 2, dtype=jnp.int32)
    columns = jnp.arange(NLON, dtype=jnp.int32)
    return jnp.mod(centre - columns, NLON).astype(jnp.int32)


def draw_land_mask(key, part):
    key = jax.random.fold_in(key, 5)
    tile_key, cell_key = jax.random.split(key)
    tile_rows = CLAT // 2
    tile_cols = CLON // 2
    levels = jax.random.randint(tile_key, (NLAT // tile_rows, NLON // tile_cols), 0, 11, dtype=jnp.int32)
    levels = jnp.maximum(levels - 2, 0)
    levels = jnp.repeat(jnp.repeat(levels, tile_rows, axis=0), tile_cols, axis=1)
    cells = jax.random.randint(cell_key, (NLAT, NLON), 0, 8, dtype=jnp.int32)
    rows = jnp.arange(NLAT, dtype=jnp.int32)[:, None]
    ocean = jnp.logical_or(cells < levels, rows >= NLAT - 2)
    return jnp.where(ocean, 1, 0).astype(jnp.int32)


def draw_cotangent(key, part):
    key = jax.random.fold_in(key, 11)
    phase_key, level_key, rough_key = jax.random.split(key, 3)
    phases = jax.random.uniform(phase_key, (2,), jnp.float32, 0.0, 2.0 * math.pi)
    rows = jnp.arange(NLAT, dtype=jnp.float32)[:, None]
    cols = jnp.arange(NLON, dtype=jnp.float32)[None, :]
    turn = 2.0 * math.pi * cols / NLON
    lat_ramp = 0.5 + rows / NLAT
    rough_env = 0.15 + 0.85 * (0.5 + 0.5 * jnp.sin(turn + phases[0]))
    smooth_shape = 0.6 - 0.4 * jnp.sin(turn + phases[0]) + 0.2 * jnp.cos(2.0 * turn + phases[1])
    rough = jnp.clip(jax.random.normal(rough_key, (L, NLAT, NLON), jnp.float32), -4.0, 4.0)
    level_scale = jax.random.uniform(level_key, (L, 1, 1), jnp.float32, 0.5, 1.5)
    smooth_amp = 0.5
    values = lat_ramp[None] * (rough_env[None] * rough + smooth_amp * smooth_shape[None] * level_scale)
    return values.astype(jnp.float32)


def plant(drawn, rng, low, largest):
    longest = drawn.shape.index(max(drawn.shape))
    spots = []
    for shift in (0, 1):
        where = [jax.random.randint(jax.random.fold_in(rng, axis), (), 0, length) for axis, length in enumerate(drawn.shape)]
        where[longest] = (where[longest] + shift) % drawn.shape[longest]
        spots.append(tuple(where))
    return drawn.at[spots[0]].set(low).at[spots[1]].set(largest)


def steps_of(own_key, extent, pieces, least, high):
    factor_of = 1.0
    for axis_at, blocks in pieces:
        heights = jax.random.uniform(jax.random.fold_in(jax.random.fold_in(own_key, 6), axis_at), (blocks,), jnp.float32, least / len(pieces), high / len(pieces))
        factor_of = factor_of * jnp.repeat(jnp.exp(heights), extent[axis_at] // blocks).reshape((-1,) + (1,) * (len(extent) - 1 - axis_at))
    return factor_of


def noise(rng, extent, spread, reach, cuts=(), kind=jnp.bfloat16):
    drawn = spread * jax.random.normal(rng, extent, jnp.float32)
    if cuts:
        drawn = drawn * steps_of(rng, extent, cuts, -0.22, 0.18)
    return jnp.clip(drawn, -reach, reach).astype(kind)


def setup_inputs(seed: int = 0, part: int = 0) -> dict:
    seeds = jax.random.split(jax.random.key(seed), 9)
    part_splits = jax.random.split(jax.random.fold_in(seeds[8], part), 9)
    state = noise(part_splits[0], (L, NLAT, NLON), 1.0, 6.0, ((1, 4), (2, 4)), jnp.float32)
    cotangent = draw_cotangent(jax.random.fold_in(jax.random.fold_in(seeds[8], part), 71), part)
    land_mask = draw_land_mask(jax.random.fold_in(seeds[8], 71), part)
    level_count = plant(jax.random.randint(seeds[3], (NLAT, NLON), 1, L + 1), jax.random.fold_in(seeds[3], 1), 1, L).astype(jnp.int32)
    fold_partner = draw_fold_partner(jax.random.fold_in(seeds[8], 71), part)
    weight_in = noise(seeds[5], (2 * L, H), (2 * L) ** -0.5, 1.0)
    weight_out = noise(seeds[6], (H, L), H ** -0.5, 0.375)
    bias_hidden = noise(seeds[7], (H,), 0.5, 3.0, (), jnp.float32)
    return {"state": state, "cotangent": cotangent, "land_mask": land_mask, "level_count": level_count, "fold_partner": fold_partner, "weight_in": weight_in, "weight_out": weight_out, "bias_hidden": bias_hidden}


DIFFUSE = 0.2
CLOSURE_STEP = 0.5

def edge_weights(mask_float, fold_partner):
    east_weight = mask_float * jnp.roll(mask_float, -1, axis=1)
    west_weight = mask_float * jnp.roll(mask_float, 1, axis=1)
    above = jnp.concatenate([mask_float[1:], mask_float[-1:][:, fold_partner]], axis=0)
    below = jnp.concatenate([jnp.zeros_like(mask_float[:1]), mask_float[:-1]], axis=0)
    return (east_weight, west_weight, mask_float * above, mask_float * below)

def laplace(grid_field, weights, fold_partner):
    east_weight, west_weight, north_weight, south_weight = weights
    east_side = jnp.roll(grid_field, -1, axis=2)
    west_side = jnp.roll(grid_field, 1, axis=2)
    north_side = jnp.concatenate([grid_field[:, 1:], grid_field[:, -1:][:, :, fold_partner]], axis=1)
    south_side = jnp.concatenate([jnp.zeros_like(grid_field[:, :1]), grid_field[:, :-1]], axis=1)
    total = east_weight * (east_side - grid_field) + west_weight * (west_side - grid_field)
    total = total + north_weight * (north_side - grid_field)
    return total + south_weight * (south_side - grid_field)

def closure_backward(features, closure_grad, weight_in, weight_out, bias_hidden):
    col_count = features.shape[2]
    block_count = features.shape[1] // 8

    def one_block(carry, index):
        feature_grad, grad_in, grad_out, grad_bias = carry
        start = (index * 8).astype(jnp.int32)
        feat_block = lax.dynamic_slice_in_dim(features, start, 8, 1).reshape(2 * L, 8 * col_count)
        grad_block = lax.dynamic_slice_in_dim(closure_grad, start, 8, 1).reshape(L, 8 * col_count)
        pre_act = jnp.dot(weight_in.T, feat_block, preferred_element_type=jnp.float32) + bias_hidden[:, None]
        activation = jnp.tanh(pre_act)
        act_half = activation.astype(jnp.bfloat16)
        back_act = jnp.dot(weight_out, grad_block, preferred_element_type=jnp.float32)
        back_pre = back_act * (1.0 - activation * activation)
        back_half = back_pre.astype(jnp.bfloat16)
        grad_out = grad_out + jnp.dot(act_half, grad_block.T, preferred_element_type=jnp.float32)
        grad_in = grad_in + jnp.dot(feat_block, back_half.T, preferred_element_type=jnp.float32)
        grad_bias = grad_bias + lax.optimization_barrier(jnp.sum(back_pre, axis=1))
        block_grad = jnp.dot(weight_in, back_half, preferred_element_type=jnp.float32).reshape(2 * L, 8, col_count)
        feature_grad = lax.dynamic_update_slice_in_dim(feature_grad, block_grad, start, 1)
        return ((feature_grad, grad_in, grad_out, grad_bias), None)
    start_carry = (jnp.zeros(features.shape, jnp.float32), jnp.zeros((2 * L, H), jnp.float32), jnp.zeros((H, L), jnp.float32), jnp.zeros((H,), jnp.float32))
    carry, _ = lax.scan(one_block, start_carry, jnp.arange(block_count, dtype=jnp.int32))
    return carry

def reference(state, cotangent, land_mask, level_count, fold_partner, weight_in, weight_out, bias_hidden):
    mask_float = land_mask.astype(jnp.float32)
    weights = edge_weights(mask_float, fold_partner)
    level_ids = jnp.arange(L, dtype=jnp.int32)[:, None, None]
    live_cells = jnp.where(level_ids < level_count[None], 1.0, 0.0).astype(jnp.float32) * mask_float[None]
    diagonal = 0.1 + 0.3 * lax.optimization_barrier(jnp.sum(live_cells, axis=0)) / L
    inv_root = 1.0 / math.sqrt(L)
    right_side = (-inv_root * lax.optimization_barrier(jnp.sum(live_cells * cotangent, axis=0)))[None]

    def operate(values):
        return diagonal * values - laplace(values, weights, fold_partner)
    pressure = jnp.zeros_like(right_side)
    residual, direction = (right_side, right_side)
    norm_now = jnp.sum(residual * residual)
    for iteration in range(ITERS):
        image = operate(direction)
        alpha = norm_now / jnp.sum(direction * image)
        pressure = pressure + alpha * direction
        residual = residual - alpha * image
        norm_next = jnp.sum(residual * residual)
        direction = residual + norm_next / norm_now * direction
        norm_now = norm_next
    adjoint_state = cotangent + inv_root * live_cells * pressure
    features = jnp.concatenate([state, laplace(state, weights, fold_partner)], axis=0).astype(jnp.bfloat16)
    closure_grad = (CLOSURE_STEP * live_cells * adjoint_state).astype(jnp.bfloat16)
    feature_grad, grad_in, grad_out, grad_bias = closure_backward(features, closure_grad, weight_in, weight_out, bias_hidden)
    adjoint_in = adjoint_state + DIFFUSE * laplace(adjoint_state, weights, fold_partner)
    adjoint_in = adjoint_in + feature_grad[:L] + laplace(feature_grad[L:], weights, fold_partner)
    scale = 1.0 / math.sqrt(NLAT * NLON)
    return (adjoint_in, grad_in * scale, grad_out * scale, grad_bias * scale)
```

```python
import functools
import math

import jax
import jax.numpy as jnp
from jax import lax
from jax.experimental import pallas as pl
from jax.experimental.pallas import tpu as pltpu
from jax.sharding import PartitionSpec as P

L = 16
H = 256
DIFFUSE = 0.2
CLOSURE_STEP = 0.5
F32 = jnp.float32
BF16 = jnp.bfloat16
MESH = pl.DeviceIdType.MESH

SHIFT = 4.25
SPAN = 4.15
TILES = 16
GROUP = 4


def fold_select(fold, lon, block, width, east_lanes, size):
    source = lax.broadcasted_iota(jnp.int32, (128, width), 0) + block * 128
    lane = lax.broadcasted_iota(jnp.int32, (128, width), 1)
    column = jnp.where(lane < east_lanes, lane, lane - 256) + lon * 128
    centre = fold[0:1, 0:1] + lon * 128
    total = source + column - centre
    hit = total == 0
    for turns in (-2, -1, 1, 2):
        hit = hit | (total == turns * size)
    return jnp.where(hit, 1.0, 0.0).astype(F32)


def exact_dot(a, b, dims=(((1,), (0,)), ((), ()))):
    return lax.dot_general(
        a, b, dims, precision=lax.Precision.HIGHEST, preferred_element_type=F32
    )


def dot_nt(a, b):
    return lax.dot_general(a, b, (((1,), (1,)), ((), ())), preferred_element_type=F32)


def krylov_coefficients(moments):
    zero = jnp.zeros_like(moments[0])

    def inner(a, b):
        total = zero
        for i, x in enumerate(a):
            for j, y in enumerate(b):
                if x is not None and y is not None:
                    total = total + x * y * moments[i + j]
        return total

    one = zero + 1.0
    residual = [one]
    direction = [one]
    pressure = [zero, zero, zero]
    norm_now = moments[0]
    for step in range(3):
        image = [SHIFT * d for d in direction] + [zero]
        image = [
            x + (SPAN * direction[k - 1] if k > 0 else zero) for k, x in enumerate(image)
        ]
        alpha = norm_now / inner(direction, image)
        alpha = jnp.minimum(jnp.maximum(alpha, 1.0 / 8.41), 10.01)
        pressure = [
            x + (alpha * direction[k] if k < len(direction) else zero)
            for k, x in enumerate(pressure)
        ]
        if step == 2:
            break
        residual = residual + [zero]
        residual = [x - alpha * y for x, y in zip(residual, image)]
        norm_next = jnp.maximum(inner(residual, residual), 0.0)
        beta = norm_next / norm_now
        direction = direction + [zero]
        direction = [x + beta * y for x, y in zip(residual, direction)]
        norm_now = norm_next
    return pressure


def kernel(
    nlat, nlon,
    state, cot, mask, count, fold, w_in, w_out, bias,
    out, g_in, g_out, g_bias,
    xt, zt, yt, feat, bext, cext, wts, basis, pres, w_in_t, bias_b, bias_acc,
    gi_acc, go_acc,
    msg, recv, diag, top, zmsg, zrecv, ztop,
    mom, mom_lat, mom_lon, gpart, g_rs, g_own, g_lon, g_full,
    e_send, e_recv, d_send, d_recv, t_send, t_recv,
    ml_send, ml_recv, mo_send, mo_recv,
    z_send, z_recv, zt_send, zt_recv,
    rs_send, rs_recv, gl_send, gl_recv, ag_send, ag_recv,
):
    rows = mask.shape[0]
    size_lon = nlon * 128
    lat = lax.axis_index("lat")
    lon = lax.axis_index("lon")
    at_top = lat == nlat - 1
    has_south = lat > 0
    has_north = lat < nlat - 1
    south = lax.rem(lat + nlat - 1, nlat)
    north = lax.rem(lat + 1, nlat)
    west = lax.rem(lon + nlon - 1, nlon)
    east = lax.rem(lon + 1, nlon)

    def lat_peer(d):
        return lax.rem(lat + d, nlat)

    def lon_peer(d):
        return lax.rem(lon + d, nlon)

    barrier = pltpu.get_barrier_semaphore()
    for d in range(1, nlat):
        pl.semaphore_signal(barrier, inc=1, device_id={"lat": lat_peer(d)}, device_id_type=MESH)
    for d in range(1, nlon):
        pl.semaphore_signal(barrier, inc=1, device_id={"lon": lon_peer(d)}, device_id_type=MESH)

    @pl.when(has_south)
    def _():
        for side in (west, east):
            pl.semaphore_signal(
                barrier, inc=1, device_id={"lat": south, "lon": side}, device_id_type=MESH
            )

    @pl.when(has_north)
    def _():
        for side in (west, east):
            pl.semaphore_signal(
                barrier, inc=1, device_id={"lat": north, "lon": side}, device_id_type=MESH
            )

    mask_f = mask[...].astype(F32)
    live_count = mask_f * count[...].astype(F32)
    total = jnp.zeros((rows, 128), F32)
    for k in range(L):
        total = total + jnp.where(live_count > k, cot[k * rows:(k + 1) * rows, :], 0.0)
    right = (-1.0 / math.sqrt(L)) * total
    bext[8:8 + rows, 0:128] = right
    cext[8:8 + rows, 0:128] = live_count
    right_t = right.T
    count_t = live_count.T

    lane = lax.broadcasted_iota(jnp.int32, (L, 128), 1)
    level = lax.broadcasted_iota(jnp.int32, (L, 128), 0).astype(F32)

    def transpose_rows(i, carry):
        low, high = carry
        for k in range(8):
            r = i * 8 + k
            x = state[pl.ds(r, L, stride=rows), :]
            xt[r + 1] = x
            low = jnp.where(lane == r, x[:, 0:1], low)
            high = jnp.where(lane == r, x[:, 127:128], high)
        return low, high

    zeros = jnp.zeros((L, 128), F32)
    low, high = lax.fori_loop(0, rows // 8, transpose_rows, (zeros, zeros))

    msg[0, 0:16] = xt[1]
    msg[0, 16:24] = right[0:8]
    msg[0, 24:32] = live_count[0:8]
    msg[1, 0:16] = xt[rows]
    msg[1, 16:24] = right[rows - 8:rows]
    msg[1, 24:32] = live_count[rows - 8:rows]
    msg[2, 0:16] = low
    msg[2, 16:24] = right_t[0:8]
    msg[2, 24:32] = count_t[0:8]
    msg[3, 0:16] = high
    msg[3, 16:24] = right_t[120:128]
    msg[3, 24:32] = count_t[120:128]

    waits = (nlat - 1) + (nlon - 1) + 2 * has_south.astype(jnp.int32) + 2 * has_north.astype(jnp.int32)
    pl.semaphore_wait(barrier, waits)

    def remote(src, dst, send, receive, device):
        return pltpu.make_async_remote_copy(
            src_ref=src, dst_ref=dst, send_sem=send, recv_sem=receive,
            device_id=device, device_id_type=MESH,
        )

    def edge_copies(source, target, send, receive):
        return (
            remote(source.at[0], target.at[1], send.at[0], receive.at[1], {"lat": south}),
            remote(source.at[1], target.at[0], send.at[1], receive.at[0], {"lat": north}),
            remote(source.at[2], target.at[3], send.at[2], receive.at[3], {"lon": west}),
            remote(source.at[3], target.at[2], send.at[3], receive.at[2], {"lon": east}),
        )

    def top_copies(source, target, send, receive):
        return [
            remote(source, target.at[d], send.at[d], receive.at[d], {"lon": lon_peer(d)})
            for d in range(1, nlon)
        ]

    def start_edges(edges, tops):
        edges[2].start()
        edges[3].start()

        @pl.when(has_south)
        def _():
            edges[0].start()

        @pl.when(has_north)
        def _():
            edges[1].start()

        @pl.when(at_top)
        def _():
            for copy in tops:
                copy.start()

    def finish_edges(edges, tops):
        edges[2].wait()
        edges[3].wait()

        @pl.when(has_south)
        def _():
            edges[0].wait_send()
            edges[1].wait_recv()

        @pl.when(has_north)
        def _():
            edges[1].wait_send()
            edges[0].wait_recv()

        @pl.when(at_top)
        def _():
            for copy in tops:
                copy.wait()

    edges = edge_copies(msg, recv, e_send, e_recv)
    tops = top_copies(msg.at[1], top, t_send, t_recv)
    corners = (
        remote(msg.at[0, 16:32], diag.at[3], d_send.at[0], d_recv.at[3], {"lat": south, "lon": west}),
        remote(msg.at[0, 16:32], diag.at[2], d_send.at[1], d_recv.at[2], {"lat": south, "lon": east}),
        remote(msg.at[1, 16:32], diag.at[1], d_send.at[2], d_recv.at[1], {"lat": north, "lon": west}),
        remote(msg.at[1, 16:32], diag.at[0], d_send.at[3], d_recv.at[0], {"lat": north, "lon": east}),
    )
    start_edges(edges, tops)

    @pl.when(has_south)
    def _():
        corners[0].start()
        corners[1].start()

    @pl.when(has_north)
    def _():
        corners[2].start()
        corners[3].start()

    pad = jnp.zeros((96, H), F32)
    w_in_t[...] = jnp.concatenate([w_in[...].astype(F32), pad], axis=0).T[:, 0:32].astype(BF16)
    bias_b[...] = jnp.broadcast_to(bias[...], (128, H)).T
    bias_acc[...] = jnp.zeros_like(bias_acc)
    gi_acc[...] = jnp.zeros_like(gi_acc)
    go_acc[...] = jnp.zeros_like(go_acc)

    finish_edges(edges, tops)

    @pl.when(has_south)
    def _():
        corners[0].wait_send()
        corners[1].wait_send()
        corners[2].wait_recv()
        corners[3].wait_recv()

    @pl.when(has_north)
    def _():
        corners[2].wait_send()
        corners[3].wait_send()
        corners[0].wait_recv()
        corners[1].wait_recv()

    middle = jnp.zeros((112, 128), F32)
    bext[8:8 + rows, 128:256] = jnp.concatenate([recv[3, 16:24], middle, recv[2, 16:24]], axis=0).T
    cext[8:8 + rows, 128:256] = jnp.concatenate([recv[3, 24:32], middle, recv[2, 24:32]], axis=0).T
    near = lax.broadcasted_iota(jnp.int32, (8, 128), 1) < 64

    @pl.when(has_south)
    def _():
        bext[0:8, 0:128] = recv[0, 16:24]
        cext[0:8, 0:128] = recv[0, 24:32]
        bext[0:8, 128:256] = jnp.where(near, diag[1, 0:8], diag[0, 0:8])
        cext[0:8, 128:256] = jnp.where(near, diag[1, 8:16], diag[0, 8:16])
        xt[0] = recv[0, 0:16]

    @pl.when(jnp.logical_not(has_south))
    def _():
        bext[0:8, :] = jnp.zeros((8, 256), F32)
        cext[0:8, :] = jnp.zeros((8, 256), F32)
        xt[0] = zeros

    last = 8 + rows

    @pl.when(has_north)
    def _():
        bext[last:last + 8, 0:128] = recv[1, 16:24]
        cext[last:last + 8, 0:128] = recv[1, 24:32]
        bext[last:last + 8, 128:256] = jnp.where(near, diag[3, 0:8], diag[2, 0:8])
        cext[last:last + 8, 128:256] = jnp.where(near, diag[3, 8:16], diag[2, 8:16])
        xt[rows + 1] = recv[1, 0:16]

    @pl.when(at_top)
    def _():
        folded = exact_dot(msg[1], fold_select(fold[...], lon, lon, 256, 192, size_lon))
        for d in range(1, nlon):
            block = lax.rem(lon + nlon - d, nlon)
            folded = folded + exact_dot(top[d], fold_select(fold[...], lon, block, 256, 192, size_lon))
        xt[rows + 1] = folded[0:16, 0:128]
        for k in range(3):
            bext[last + k:last + k + 1, :] = folded[23 - k:24 - k, :]
            cext[last + k:last + k + 1, :] = folded[31 - k:32 - k, :]
        bext[last + 3:last + 8, :] = jnp.zeros((5, 256), F32)
        cext[last + 3:last + 8, :] = jnp.zeros((5, 256), F32)

    ext = rows + 16
    counts = cext[...]
    ocean = jnp.where(counts > 0.5, 1.0, 0.0).astype(F32)

    def sides(v):
        return (
            pltpu.roll(v, 255, 1), pltpu.roll(v, 1, 1),
            pltpu.roll(v, ext - 1, 0), pltpu.roll(v, 1, 0),
        )

    weights = [ocean * side for side in sides(ocean)]
    weight_sum = weights[0] + weights[1] + weights[2] + weights[3]
    for k in range(4):
        wts[k] = weights[k][8:8 + rows, 0:128]
    wts[4] = weight_sum[8:8 + rows, 0:128]
    wts[5] = live_count
    inv = 1.0 / SPAN
    centre_weight = ((0.1 - SHIFT) + (0.3 / L) * counts + weight_sum) * inv
    weights = [w * inv for w in weights]

    def shifted(v):
        side = sides(v)
        r = centre_weight * v
        for k in range(4):
            r = r - weights[k] * side[k]
        return r

    def own(v):
        return v[8:8 + rows, 0:128]

    def colsum(a, b):
        return jnp.sum(a * b, axis=0, keepdims=True)

    u0 = bext[...]
    u1 = shifted(u0)
    u2 = shifted(u1)
    u3 = own(shifted(u2))
    u0, u1, u2 = own(u0), own(u1), own(u2)
    basis[0] = u0
    basis[1] = u1
    basis[2] = u2
    mom[...] = jnp.concatenate(
        [colsum(u0, u0), colsum(u0, u1), colsum(u1, u1), colsum(u1, u2),
         colsum(u2, u2), colsum(u2, u3), jnp.zeros((2, 128), F32)], axis=0
    )

    mom_lat_copies = [
        remote(mom, mom_lat.at[d], ml_send.at[d], ml_recv.at[d], {"lat": lat_peer(d)})
        for d in range(1, nlat)
    ]
    for copy in mom_lat_copies:
        copy.start()

    def lap_row(field, ghost_west, ghost_east, r):
        x = field[r + 1]
        e = jnp.where(lane == 127, pltpu.roll(ghost_east, 127 - r, 1), pltpu.roll(x, 127, 1))
        w = jnp.where(lane == 0, pltpu.roll(ghost_west, lax.rem(128 - r, 128), 1), pltpu.roll(x, 1, 1))
        res = wts[0, pl.ds(r, 1), :] * e + wts[1, pl.ds(r, 1), :] * w
        res = res + wts[2, pl.ds(r, 1), :] * field[r + 2]
        res = res + wts[3, pl.ds(r, 1), :] * field[r]
        return res - wts[4, pl.ds(r, 1), :] * x

    ghost_w = recv[2, 0:16]
    ghost_e = recv[3, 0:16]

    def feature_rows(i, carry):
        for k in range(4):
            r = i * 4 + k
            lap = lap_row(xt, ghost_w, ghost_e, r)
            feat[r] = jnp.concatenate([xt[r + 1], lap], axis=0).astype(BF16)
        return carry

    lax.fori_loop(0, rows // 8, feature_rows, 0)
    for copy in mom_lat_copies:
        copy.wait()
    part = mom[...]
    for d in range(1, nlat):
        part = part + mom_lat[d]
    mom_lon[0] = part
    mom_lon_copies = [
        remote(mom_lon.at[0], mom_lon.at[d], mo_send.at[d], mo_recv.at[d], {"lon": lon_peer(d)})
        for d in range(1, nlon)
    ]
    for copy in mom_lon_copies:
        copy.start()
    lax.fori_loop(rows // 8, rows // 4, feature_rows, 0)
    for copy in mom_lon_copies:
        copy.wait()
    part = mom_lon[0]
    for d in range(1, nlon):
        part = part + mom_lon[d]
    sums = jnp.sum(part, axis=1, keepdims=True)
    coefficients = krylov_coefficients([sums[k:k + 1, :] for k in range(6)])
    scale = 1.0 / math.sqrt(L)
    pres[...] = scale * (
        coefficients[0] * basis[0] + coefficients[1] * basis[1] + coefficients[2] * basis[2]
    )

    def closure(i, carry):
        low, high = carry
        adjoints, grads, feats = [], [], []
        for k in range(GROUP):
            r = i * GROUP + k
            live = level < wts[5, pl.ds(r, 1), :]
            adj = cot[pl.ds(r, L, stride=rows), :] + jnp.where(live, pres[pl.ds(r, 1), :], 0.0)
            adjoints.append(adj)
            grads.append(jnp.where(live, CLOSURE_STEP * adj, 0.0).astype(BF16))
            feats.append(feat[r])
        features = jnp.concatenate(feats, axis=1)
        grad = jnp.concatenate(grads, axis=1)
        bias_tile = jnp.concatenate([bias_b[...]] * GROUP, axis=1)
        act = jnp.tanh(jnp.dot(w_in_t[...], features, preferred_element_type=F32) + bias_tile)
        back = jnp.dot(w_out[...], grad, preferred_element_type=F32)
        pre = back * (1.0 - act * act)
        half = pre.astype(BF16)
        acc = pre[:, 0:128]
        for k in range(1, GROUP):
            acc = acc + pre[:, k * 128:(k + 1) * 128]
        bias_acc[...] += acc
        gi_acc[...] += dot_nt(features, half)
        go_acc[...] += dot_nt(grad, act.astype(BF16))
        fg = jnp.dot(w_in[...], half, preferred_element_type=F32)
        for k in range(GROUP):
            r = i * GROUP + k
            z = DIFFUSE * adjoints[k] + fg[16:32, k * 128:(k + 1) * 128]
            zt[r + 1] = z
            yt[r] = adjoints[k] + fg[0:16, k * 128:(k + 1) * 128]
            low = jnp.where(lane == r, z[:, 0:1], low)
            high = jnp.where(lane == r, z[:, 127:128], high)
        return low, high

    low, high = lax.fori_loop(0, rows // GROUP, closure, (zeros, zeros))

    zmsg[0] = zt[1]
    zmsg[1] = zt[rows]
    zmsg[2] = low
    zmsg[3] = high
    z_edges = edge_copies(zmsg, zrecv, z_send, z_recv)
    z_tops = top_copies(zmsg.at[1], ztop, zt_send, zt_recv)
    start_edges(z_edges, z_tops)

    share = TILES // nlat
    ones = jnp.full((8, 128), 1.0, F32)
    bias_rows = exact_dot(ones, bias_acc[...], (((1,), (1,)), ((), ())))
    for half_at in range(2):
        cols = slice(half_at * 128, half_at * 128 + 128)
        for t in range(4):
            gpart[half_at * 8 + t] = gi_acc[t * 8:t * 8 + 8, cols]
        for t in range(2):
            gpart[half_at * 8 + 4 + t] = go_acc[t * 8:t * 8 + 8, cols]
        gpart[half_at * 8 + 6] = bias_rows[:, cols]
        gpart[half_at * 8 + 7] = jnp.zeros((8, 128), F32)

    rs_copies = [
        remote(
            gpart.at[pl.ds(lat_peer(d) * share, share)], g_rs.at[d],
            rs_send.at[d], rs_recv.at[d], {"lat": lat_peer(d)},
        )
        for d in range(1, nlat)
    ]
    for copy in rs_copies:
        copy.start()
    for copy in rs_copies:
        copy.wait()
    mine = gpart[pl.ds(lat * share, share)]
    for d in range(1, nlat):
        mine = mine + g_rs[d]
    g_lon[0] = mine
    gl_copies = [
        remote(g_lon.at[0], g_lon.at[d], gl_send.at[d], gl_recv.at[d], {"lon": lon_peer(d)})
        for d in range(1, nlon)
    ]
    for copy in gl_copies:
        copy.start()

    finish_edges(z_edges, z_tops)

    @pl.when(has_south)
    def _():
        zt[0] = zrecv[0]

    @pl.when(jnp.logical_not(has_south))
    def _():
        zt[0] = zeros

    @pl.when(has_north)
    def _():
        zt[rows + 1] = zrecv[1]

    @pl.when(at_top)
    def _():
        folded = exact_dot(zmsg[1], fold_select(fold[...], lon, lon, 128, 192, size_lon))
        for d in range(1, nlon):
            block = lax.rem(lon + nlon - d, nlon)
            folded = folded + exact_dot(ztop[d], fold_select(fold[...], lon, block, 128, 192, size_lon))
        zt[rows + 1] = folded

    z_west = zrecv[2]
    z_east = zrecv[3]

    def final_rows(i, carry):
        for k in range(4):
            r = i * 4 + k
            out[pl.ds(r, L, stride=rows), :] = yt[r] + lap_row(zt, z_west, z_east, r)
        return carry

    lax.fori_loop(0, rows // 8, final_rows, 0)
    for copy in gl_copies:
        copy.wait()
    mine = g_lon[0]
    for d in range(1, nlon):
        mine = mine + g_lon[d]
    grad_scale = 1.0 / math.sqrt(rows * nlat * 128 * nlon)
    g_own[...] = mine * grad_scale
    g_full[pl.ds(lat * share, share)] = g_own[...]
    ag_copies = [
        remote(
            g_own, g_full.at[pl.ds(lat * share, share)],
            ag_send.at[d], ag_recv.at[d], {"lat": lat_peer(d)},
        )
        for d in range(1, nlat)
    ]
    for copy in ag_copies:
        copy.start()
    lax.fori_loop(rows // 8, rows // 4, final_rows, 0)
    for copy in ag_copies:
        copy.wait()
    for half_at in range(2):
        cols = slice(half_at * 128, half_at * 128 + 128)
        for t in range(4):
            g_in[t * 8:t * 8 + 8, cols] = g_full[half_at * 8 + t]
        block = jnp.concatenate(
            [g_full[half_at * 8 + 4], g_full[half_at * 8 + 5], jnp.zeros((112, 128), F32)], axis=0
        )
        g_out[half_at * 128:half_at * 128 + 128, :] = block.T[:, 0:16]
        g_bias[0:1, cols] = g_full[half_at * 8 + 6, 0:1, :]


def on_device(nlat, nlon, state, cotangent, land_mask, level_count, fold_partner, weight_in, weight_out, bias_hidden):
    rows, cols = land_mask.shape
    vm = pltpu.VMEM
    dma = pltpu.SemaphoreType.DMA
    share = TILES // nlat
    scratch = [
        vm((rows + 2, L, 128), F32), vm((rows + 2, L, 128), F32), vm((rows, L, 128), F32),
        vm((rows, 2 * L, 128), BF16), vm((rows + 16, 256), F32), vm((rows + 16, 256), F32),
        vm((6, rows, 128), F32), vm((3, rows, 128), F32), vm((rows, 128), F32),
        vm((H, 2 * L), BF16), vm((H, 128), F32), vm((H, 128), F32),
        vm((2 * L, H), F32), vm((L, H), F32),
        vm((4, 32, 128), F32), vm((4, 32, 128), F32), vm((4, 16, 128), F32), vm((nlon, 32, 128), F32),
        vm((4, L, 128), F32), vm((4, L, 128), F32), vm((nlon, L, 128), F32),
        vm((8, 128), F32), vm((nlat, 8, 128), F32), vm((nlon, 8, 128), F32),
        vm((TILES, 8, 128), F32), vm((nlat, share, 8, 128), F32), vm((share, 8, 128), F32),
        vm((nlon, share, 8, 128), F32), vm((TILES, 8, 128), F32),
        dma((4,)), dma((4,)), dma((4,)), dma((4,)), dma((nlon,)), dma((nlon,)),
        dma((nlat,)), dma((nlat,)), dma((nlon,)), dma((nlon,)),
        dma((4,)), dma((4,)), dma((nlon,)), dma((nlon,)),
        dma((nlat,)), dma((nlat,)), dma((nlon,)), dma((nlon,)), dma((nlat,)), dma((nlat,)),
    ]
    spec = pl.BlockSpec(memory_space=pltpu.VMEM)
    out, g_in, g_out, g_bias = pl.pallas_call(
        functools.partial(kernel, nlat, nlon),
        out_shape=(
            jax.ShapeDtypeStruct((L * rows, cols), F32),
            jax.ShapeDtypeStruct((2 * L, H), F32),
            jax.ShapeDtypeStruct((H, L), F32),
            jax.ShapeDtypeStruct((1, H), F32),
        ),
        in_specs=[spec] * 8,
        out_specs=(spec,) * 4,
        scratch_shapes=scratch,
        compiler_params=pltpu.CompilerParams(
            collective_id=0, has_side_effects=True, vmem_limit_bytes=40 * 1024 * 1024
        ),
    )(
        state.reshape(L * rows, cols), cotangent.reshape(L * rows, cols), land_mask, level_count,
        fold_partner.reshape(1, cols), weight_in, weight_out, bias_hidden.reshape(1, H),
    )
    return out.reshape(L, rows, cols), g_in, g_out, g_bias.reshape(H)


def solution(mesh):
    placed = (
        P("ens", "lat", "lon"), P("ens", "lat", "lon"), P("lat", "lon"), P("lat", "lon"),
        P("lon"), P(), P(), P(),
    )
    body = functools.partial(on_device, mesh.shape["lat"], mesh.shape["lon"])
    return jax.shard_map(
        body,
        mesh=mesh,
        in_specs=placed,
        out_specs=(P("ens", "lat", "lon"), P("ens", None), P("ens", None), P("ens")),
        check_vma=False,
    )
```

```python
import functools
import math

import jax
import jax.numpy as jnp
from jax import lax
from jax.experimental import pallas as pl
from jax.experimental.pallas import tpu as pltpu
from jax.sharding import PartitionSpec as P

L = 16
H = 256
DIFFUSE = 0.2
CLOSURE_STEP = 0.5
F32 = jnp.float32
BF16 = jnp.bfloat16
MESH = pl.DeviceIdType.MESH

SHIFT = 4.25
SPAN = 4.15
TILES = 16
GROUP = 16


def fold_select(fold, lon, block, width, east_lanes, size):
    source = lax.broadcasted_iota(jnp.int32, (128, width), 0) + block * 128
    lane = lax.broadcasted_iota(jnp.int32, (128, width), 1)
    column = jnp.where(lane < east_lanes, lane, lane - 256) + lon * 128
    centre = fold[0:1, 0:1] + lon * 128
    total = source + column - centre
    hit = total == 0
    for turns in (-2, -1, 1, 2):
        hit = hit | (total == turns * size)
    return jnp.where(hit, 1.0, 0.0).astype(F32)


def exact_dot(a, b, dims=(((1,), (0,)), ((), ()))):
    return lax.dot_general(
        a, b, dims, precision=lax.Precision.HIGHEST, preferred_element_type=F32
    )


def dot_nt(a, b):
    return lax.dot_general(a, b, (((1,), (1,)), ((), ())), preferred_element_type=F32)


def krylov_coefficients(moments):
    zero = jnp.zeros_like(moments[0])

    def inner(a, b):
        total = zero
        for i, x in enumerate(a):
            for j, y in enumerate(b):
                if x is not None and y is not None:
                    total = total + x * y * moments[i + j]
        return total

    one = zero + 1.0
    residual = [one]
    direction = [one]
    pressure = [zero, zero, zero]
    norm_now = moments[0]
    for step in range(3):
        image = [SHIFT * d for d in direction] + [zero]
        image = [
            x + (SPAN * direction[k - 1] if k > 0 else zero) for k, x in enumerate(image)
        ]
        alpha = norm_now / inner(direction, image)
        alpha = jnp.minimum(jnp.maximum(alpha, 1.0 / 8.41), 10.01)
        pressure = [
            x + (alpha * direction[k] if k < len(direction) else zero)
            for k, x in enumerate(pressure)
        ]
        if step == 2:
            break
        residual = residual + [zero]
        residual = [x - alpha * y for x, y in zip(residual, image)]
        norm_next = jnp.maximum(inner(residual, residual), 0.0)
        beta = norm_next / norm_now
        direction = direction + [zero]
        direction = [x + beta * y for x, y in zip(residual, direction)]
        norm_now = norm_next
    return pressure


def kernel(
    nlat, nlon,
    state_h, cot_h, mask_h, count_h, fold, w_in, w_out_t, bias,
    out, g_in, g_out, g_bias,
    state, cot, mask, count, load_sem,
    xt, zt, yt, feat, bext, cext, wts, basis, pres, w_in_t, w_out_b, bias_b, bias_acc,
    gi_acc, go_acc,
    msg, recv, diag, top, zmsg, zrecv, ztop,
    mom, mom_in, gpart, g_rs, g_own, g_full,
    e_send, e_recv, d_send, d_recv, t_send, t_recv,
    m_send, m_recv,
    z_send, z_recv, zt_send, zt_recv,
    rs_send, rs_recv, ag_send, ag_recv,
):
    rows = mask.shape[0]
    size_lon = nlon * 128
    lat = lax.axis_index("lat")
    lon = lax.axis_index("lon")
    at_top = lat == nlat - 1
    has_south = lat > 0
    has_north = lat < nlat - 1
    south = lax.rem(lat + nlat - 1, nlat)
    north = lax.rem(lat + 1, nlat)
    west = lax.rem(lon + nlon - 1, nlon)
    east = lax.rem(lon + 1, nlon)

    def lon_peer(d):
        return lax.rem(lon + d, nlon)

    group = nlat * nlon
    me = lon * nlat + lat

    def peer_index(d):
        return lax.rem(me + d, group)

    def peer(d):
        index = peer_index(d)
        return {"lat": lax.rem(index, nlat), "lon": index // nlat}

    loads = [
        pltpu.make_async_copy(source, target, load_sem.at[k])
        for k, (source, target) in enumerate(
            ((mask_h, mask), (count_h, count), (cot_h, cot), (state_h, state))
        )
    ]
    for load in loads:
        load.start()
    barrier = pltpu.get_barrier_semaphore()
    for d in range(1, group):
        pl.semaphore_signal(barrier, inc=1, device_id=peer(d), device_id_type=MESH)
    for load in loads[:3]:
        load.wait()

    mask_f = mask[...].astype(F32)
    live_count = mask_f * count[...].astype(F32)
    total = jnp.zeros((rows, 128), F32)
    for k in range(L):
        total = total + jnp.where(live_count > k, cot[k * rows:(k + 1) * rows, :], 0.0)
    right = (-1.0 / math.sqrt(L)) * total
    bext[8:8 + rows, 0:128] = right
    cext[8:8 + rows, 0:128] = live_count
    right_t = right.T
    count_t = live_count.T

    lane = lax.broadcasted_iota(jnp.int32, (L, 128), 1)
    level = lax.broadcasted_iota(jnp.int32, (L, 128), 0).astype(F32)

    def transpose_rows(i, carry):
        low, high = carry
        for k in range(8):
            r = i * 8 + k
            x = state[pl.ds(r, L, stride=rows), :]
            xt[r + 1] = x
            low = jnp.where(lane == r, x[:, 0:1], low)
            high = jnp.where(lane == r, x[:, 127:128], high)
        return low, high

    zeros = jnp.zeros((L, 128), F32)
    loads[3].wait()
    low, high = lax.fori_loop(0, rows // 8, transpose_rows, (zeros, zeros))

    msg[0, 0:16] = xt[1]
    msg[0, 16:24] = right[0:8]
    msg[0, 24:32] = live_count[0:8]
    msg[1, 0:16] = xt[rows]
    msg[1, 16:24] = right[rows - 8:rows]
    msg[1, 24:32] = live_count[rows - 8:rows]
    msg[2, 0:16] = low
    msg[2, 16:24] = right_t[0:8]
    msg[2, 24:32] = count_t[0:8]
    msg[3, 0:16] = high
    msg[3, 16:24] = right_t[120:128]
    msg[3, 24:32] = count_t[120:128]

    pl.semaphore_wait(barrier, group - 1)

    def remote(src, dst, send, receive, device):
        return pltpu.make_async_remote_copy(
            src_ref=src, dst_ref=dst, send_sem=send, recv_sem=receive,
            device_id=device, device_id_type=MESH,
        )

    def edge_copies(source, target, send, receive):
        return (
            remote(source.at[0], target.at[1], send.at[0], receive.at[1], {"lat": south}),
            remote(source.at[1], target.at[0], send.at[1], receive.at[0], {"lat": north}),
            remote(source.at[2], target.at[3], send.at[2], receive.at[3], {"lon": west}),
            remote(source.at[3], target.at[2], send.at[3], receive.at[2], {"lon": east}),
        )

    def top_copies(source, target, send, receive):
        return [
            remote(source, target.at[d], send.at[d], receive.at[d], {"lon": lon_peer(d)})
            for d in range(1, nlon)
        ]

    def start_edges(edges, tops):
        edges[2].start()
        edges[3].start()

        @pl.when(has_south)
        def _():
            edges[0].start()

        @pl.when(has_north)
        def _():
            edges[1].start()

        @pl.when(at_top)
        def _():
            for copy in tops:
                copy.start()

    def finish_edges(edges, tops):
        edges[2].wait()
        edges[3].wait()

        @pl.when(has_south)
        def _():
            edges[0].wait_send()
            edges[1].wait_recv()

        @pl.when(has_north)
        def _():
            edges[1].wait_send()
            edges[0].wait_recv()

        @pl.when(at_top)
        def _():
            for copy in tops:
                copy.wait()

    edges = edge_copies(msg, recv, e_send, e_recv)
    tops = top_copies(msg.at[1], top, t_send, t_recv)
    corners = (
        remote(msg.at[0, 16:32], diag.at[3], d_send.at[0], d_recv.at[3], {"lat": south, "lon": west}),
        remote(msg.at[0, 16:32], diag.at[2], d_send.at[1], d_recv.at[2], {"lat": south, "lon": east}),
        remote(msg.at[1, 16:32], diag.at[1], d_send.at[2], d_recv.at[1], {"lat": north, "lon": west}),
        remote(msg.at[1, 16:32], diag.at[0], d_send.at[3], d_recv.at[0], {"lat": north, "lon": east}),
    )
    start_edges(edges, tops)

    @pl.when(has_south)
    def _():
        corners[0].start()
        corners[1].start()

    @pl.when(has_north)
    def _():
        corners[2].start()
        corners[3].start()

    pad = jnp.zeros((96, H), F32)
    w_in_t[...] = jnp.concatenate([w_in[...].astype(F32), pad], axis=0).T[:, 0:32].astype(BF16)
    w_out_b[...] = jnp.concatenate(
        [w_out_t[...].astype(F32), jnp.zeros((112, H), F32)], axis=0
    ).T[:, 0:L].astype(BF16)
    bias_b[...] = jnp.broadcast_to(bias[...], (128, H)).T
    bias_acc[...] = jnp.zeros_like(bias_acc)
    gi_acc[...] = jnp.zeros_like(gi_acc)
    go_acc[...] = jnp.zeros_like(go_acc)

    finish_edges(edges, tops)

    @pl.when(has_south)
    def _():
        corners[0].wait_send()
        corners[1].wait_send()
        corners[2].wait_recv()
        corners[3].wait_recv()

    @pl.when(has_north)
    def _():
        corners[2].wait_send()
        corners[3].wait_send()
        corners[0].wait_recv()
        corners[1].wait_recv()

    middle = jnp.zeros((112, 128), F32)
    bext[8:8 + rows, 128:256] = jnp.concatenate([recv[3, 16:24], middle, recv[2, 16:24]], axis=0).T
    cext[8:8 + rows, 128:256] = jnp.concatenate([recv[3, 24:32], middle, recv[2, 24:32]], axis=0).T
    near = lax.broadcasted_iota(jnp.int32, (8, 128), 1) < 64

    @pl.when(has_south)
    def _():
        bext[0:8, 0:128] = recv[0, 16:24]
        cext[0:8, 0:128] = recv[0, 24:32]
        bext[0:8, 128:256] = jnp.where(near, diag[1, 0:8], diag[0, 0:8])
        cext[0:8, 128:256] = jnp.where(near, diag[1, 8:16], diag[0, 8:16])
        xt[0] = recv[0, 0:16]

    @pl.when(jnp.logical_not(has_south))
    def _():
        bext[0:8, :] = jnp.zeros((8, 256), F32)
        cext[0:8, :] = jnp.zeros((8, 256), F32)
        xt[0] = zeros

    last = 8 + rows

    @pl.when(has_north)
    def _():
        bext[last:last + 8, 0:128] = recv[1, 16:24]
        cext[last:last + 8, 0:128] = recv[1, 24:32]
        bext[last:last + 8, 128:256] = jnp.where(near, diag[3, 0:8], diag[2, 0:8])
        cext[last:last + 8, 128:256] = jnp.where(near, diag[3, 8:16], diag[2, 8:16])
        xt[rows + 1] = recv[1, 0:16]

    @pl.when(at_top)
    def _():
        folded = exact_dot(msg[1], fold_select(fold[...], lon, lon, 256, 192, size_lon))
        for d in range(1, nlon):
            block = lax.rem(lon + nlon - d, nlon)
            folded = folded + exact_dot(top[d], fold_select(fold[...], lon, block, 256, 192, size_lon))
        xt[rows + 1] = folded[0:16, 0:128]
        for k in range(3):
            bext[last + k:last + k + 1, :] = folded[23 - k:24 - k, :]
            cext[last + k:last + k + 1, :] = folded[31 - k:32 - k, :]
        bext[last + 3:last + 8, :] = jnp.zeros((5, 256), F32)
        cext[last + 3:last + 8, :] = jnp.zeros((5, 256), F32)

    ext = rows + 16
    counts = cext[...]
    ocean = jnp.where(counts > 0.5, 1.0, 0.0).astype(F32)

    def sides(v):
        return (
            pltpu.roll(v, 255, 1), pltpu.roll(v, 1, 1),
            pltpu.roll(v, ext - 1, 0), pltpu.roll(v, 1, 0),
        )

    weights = [ocean * side for side in sides(ocean)]
    weight_sum = weights[0] + weights[1] + weights[2] + weights[3]
    for k in range(4):
        wts[k] = weights[k][8:8 + rows, 0:128]
    wts[4] = weight_sum[8:8 + rows, 0:128]
    wts[5] = live_count
    inv = 1.0 / SPAN
    centre_weight = ((0.1 - SHIFT) + (0.3 / L) * counts + weight_sum) * inv
    weights = [w * inv for w in weights]

    def shifted(v):
        side = sides(v)
        r = centre_weight * v
        for k in range(4):
            r = r - weights[k] * side[k]
        return r

    def own(v):
        return v[8:8 + rows, 0:128]

    def colsum(a, b):
        return jnp.sum(a * b, axis=0, keepdims=True)

    u0 = bext[...]
    u1 = shifted(u0)
    u2 = shifted(u1)
    u3 = own(shifted(u2))
    u0, u1, u2 = own(u0), own(u1), own(u2)
    basis[0] = u0
    basis[1] = u1
    basis[2] = u2
    mom[...] = jnp.concatenate(
        [colsum(u0, u0), colsum(u0, u1), colsum(u1, u1), colsum(u1, u2),
         colsum(u2, u2), colsum(u2, u3), jnp.zeros((2, 128), F32)], axis=0
    )

    mom_copies = [
        remote(mom, mom_in.at[d], m_send.at[d], m_recv.at[d], peer(d)) for d in range(1, group)
    ]
    for copy in mom_copies:
        copy.start()

    def lap_row(field, ghost_west, ghost_east, r):
        x = field[r + 1]
        e = jnp.where(lane == 127, pltpu.roll(ghost_east, 127 - r, 1), pltpu.roll(x, 127, 1))
        w = jnp.where(lane == 0, pltpu.roll(ghost_west, lax.rem(128 - r, 128), 1), pltpu.roll(x, 1, 1))
        res = wts[0, pl.ds(r, 1), :] * e + wts[1, pl.ds(r, 1), :] * w
        res = res + wts[2, pl.ds(r, 1), :] * field[r + 2]
        res = res + wts[3, pl.ds(r, 1), :] * field[r]
        return res - wts[4, pl.ds(r, 1), :] * x

    ghost_w = recv[2, 0:16]
    ghost_e = recv[3, 0:16]

    def feature_rows(i, carry):
        for k in range(16):
            r = i * 16 + k
            lap = lap_row(xt, ghost_w, ghost_e, r)
            both = jnp.concatenate([xt[r + 1], lap], axis=0)
            feat[r] = both.astype(BF16)
        return carry

    lax.fori_loop(0, rows // 16, feature_rows, 0)
    for copy in mom_copies:
        copy.wait()
    part = mom[...]
    for d in range(1, group):
        part = part + mom_in[d]
    sums = jnp.sum(part, axis=1, keepdims=True)
    coefficients = krylov_coefficients([sums[k:k + 1, :] for k in range(6)])
    scale = 1.0 / math.sqrt(L)
    pres[...] = scale * (
        coefficients[0] * basis[0] + coefficients[1] * basis[1] + coefficients[2] * basis[2]
    )

    def closure(i, carry):
        low, high = carry
        adjoints, grads, feats = [], [], []
        for k in range(GROUP):
            r = i * GROUP + k
            live = level < wts[5, pl.ds(r, 1), :]
            adj = cot[pl.ds(r, L, stride=rows), :] + jnp.where(live, pres[pl.ds(r, 1), :], 0.0)
            grad = jnp.where(live, CLOSURE_STEP * adj, 0.0)
            adjoints.append(adj)
            grads.append(grad.astype(BF16))
            feats.append(feat[r])
        features = jnp.concatenate(feats, axis=1)
        grad = jnp.concatenate(grads, axis=1)
        bias_tile = jnp.concatenate([bias_b[...]] * GROUP, axis=1)
        act = jnp.tanh(jnp.dot(w_in_t[...], features, preferred_element_type=F32) + bias_tile)
        back = jnp.dot(w_out_b[...], grad, preferred_element_type=F32)
        pre = back * (1.0 - act * act)
        half = pre.astype(BF16)
        acc = pre[:, 0:128]
        for k in range(1, GROUP):
            acc = acc + pre[:, k * 128:(k + 1) * 128]
        bias_acc[...] += acc
        gi_acc[...] += dot_nt(features, half)
        go_acc[...] += dot_nt(grad, act.astype(BF16))
        fg = jnp.dot(w_in[...], half, preferred_element_type=F32)
        for k in range(GROUP):
            r = i * GROUP + k
            z = DIFFUSE * adjoints[k] + fg[16:32, k * 128:(k + 1) * 128]
            zt[r + 1] = z
            yt[r] = adjoints[k] + fg[0:16, k * 128:(k + 1) * 128]
            low = jnp.where(lane == r, z[:, 0:1], low)
            high = jnp.where(lane == r, z[:, 127:128], high)
        return low, high

    low, high = lax.fori_loop(0, rows // GROUP, closure, (zeros, zeros))

    zmsg[0] = zt[1]
    zmsg[1] = zt[rows]
    zmsg[2] = low
    zmsg[3] = high
    z_edges = edge_copies(zmsg, zrecv, z_send, z_recv)
    z_tops = top_copies(zmsg.at[1], ztop, zt_send, zt_recv)
    start_edges(z_edges, z_tops)

    bias_rows = exact_dot(jnp.full((8, 128), 1.0, F32), bias_acc[...], (((1,), (1,)), ((), ())))
    for half_at in range(2):
        cols = slice(half_at * 128, half_at * 128 + 128)
        for t in range(4):
            gpart[half_at * 8 + t] = gi_acc[t * 8:t * 8 + 8, cols]
        for t in range(2):
            gpart[half_at * 8 + 4 + t] = go_acc[t * 8:t * 8 + 8, cols]
        gpart[half_at * 8 + 6] = bias_rows[:, cols]
        gpart[half_at * 8 + 7] = jnp.zeros((8, 128), F32)

    owner = me < TILES
    my_tile = lax.rem(me, TILES)
    rs_copies = [
        remote(
            gpart.at[lax.rem(peer_index(d), TILES)], g_rs.at[d],
            rs_send.at[d], rs_recv.at[d], peer(d),
        )
        for d in range(1, group)
    ]
    ag_copies = [
        remote(g_own, g_full.at[my_tile], ag_send.at[d], ag_recv.at[d], peer(d))
        for d in range(1, group)
    ]
    all_own = group <= TILES

    def guarded(condition, action):
        if all_own:
            action()
        else:
            pl.when(condition)(action)

    for d, copy in enumerate(rs_copies, 1):
        guarded(peer_index(d) < TILES, copy.start)
    for d, copy in enumerate(rs_copies, 1):
        guarded(peer_index(d) < TILES, copy.wait_send)
        guarded(owner, copy.wait_recv)

    def share_tile():
        mine = gpart[my_tile]
        for d in range(1, group):
            mine = mine + g_rs[d]
        g_own[...] = mine * (1.0 / math.sqrt(rows * nlat * 128 * nlon))
        g_full[my_tile] = g_own[...]
        for copy in ag_copies:
            copy.start()

    guarded(owner, share_tile)

    finish_edges(z_edges, z_tops)

    @pl.when(has_south)
    def _():
        zt[0] = zrecv[0]

    @pl.when(jnp.logical_not(has_south))
    def _():
        zt[0] = zeros

    @pl.when(has_north)
    def _():
        zt[rows + 1] = zrecv[1]

    @pl.when(at_top)
    def _():
        folded = exact_dot(zmsg[1], fold_select(fold[...], lon, lon, 128, 192, size_lon))
        for d in range(1, nlon):
            block = lax.rem(lon + nlon - d, nlon)
            folded = folded + exact_dot(ztop[d], fold_select(fold[...], lon, block, 128, 192, size_lon))
        zt[rows + 1] = folded

    z_west = zrecv[2]
    z_east = zrecv[3]

    def final_rows(i, carry):
        for k in range(16):
            r = i * 16 + k
            out[pl.ds(r, L, stride=rows), :] = yt[r] + lap_row(zt, z_west, z_east, r)
        return carry

    lax.fori_loop(0, rows // 16, final_rows, 0)
    for d, copy in enumerate(ag_copies, 1):
        guarded(owner, copy.wait_send)
        guarded(lax.rem(me + group - d, group) < TILES, copy.wait_recv)
    for half_at in range(2):
        cols = slice(half_at * 128, half_at * 128 + 128)
        for t in range(4):
            g_in[t * 8:t * 8 + 8, cols] = g_full[half_at * 8 + t]
        for t in range(2):
            g_out[t * 8:t * 8 + 8, cols] = g_full[half_at * 8 + 4 + t]
        g_bias[0:1, cols] = g_full[half_at * 8 + 6, 0:1, :]


def on_device(nlat, nlon, state, cotangent, land_mask, level_count, fold_partner, weight_in, weight_out, bias_hidden):
    rows, cols = land_mask.shape
    group = nlat * nlon
    vm = pltpu.VMEM
    dma = pltpu.SemaphoreType.DMA
    scratch = [
        vm((L * rows, 128), F32), vm((L * rows, 128), F32),
        vm((rows, 128), jnp.int32), vm((rows, 128), jnp.int32), dma((4,)),
        vm((rows + 2, L, 128), F32), vm((rows + 2, L, 128), F32), vm((rows, L, 128), F32),
        vm((rows, 2 * L, 128), BF16),
        vm((rows + 16, 256), F32), vm((rows + 16, 256), F32),
        vm((6, rows, 128), F32), vm((3, rows, 128), F32), vm((rows, 128), F32),
        vm((H, 2 * L), BF16), vm((H, L), BF16), vm((H, 128), F32), vm((H, 128), F32),
        vm((2 * L, H), F32), vm((L, H), F32),
        vm((4, 32, 128), F32), vm((4, 32, 128), F32), vm((4, 16, 128), F32), vm((nlon, 32, 128), F32),
        vm((4, L, 128), F32), vm((4, L, 128), F32), vm((nlon, L, 128), F32),
        vm((8, 128), F32), vm((group, 8, 128), F32),
        vm((TILES, 8, 128), F32), vm((group, 8, 128), F32), vm((8, 128), F32),
        vm((TILES, 8, 128), F32),
        dma((4,)), dma((4,)), dma((4,)), dma((4,)), dma((nlon,)), dma((nlon,)),
        dma((group,)), dma((group,)),
        dma((4,)), dma((4,)), dma((nlon,)), dma((nlon,)),
        dma((group,)), dma((group,)), dma((group,)), dma((group,)),
    ]
    spec = pl.BlockSpec(memory_space=pltpu.VMEM)
    hbm = pl.BlockSpec(memory_space=pltpu.HBM)
    shapes = (
        jax.ShapeDtypeStruct((L * rows, cols), F32),
        jax.ShapeDtypeStruct((2 * L, H), F32),
        jax.ShapeDtypeStruct((L, H), F32),
        jax.ShapeDtypeStruct((1, H), F32),
    )
    out, g_in, g_out, g_bias = pl.pallas_call(
        functools.partial(kernel, nlat, nlon),
        out_shape=shapes,
        in_specs=[hbm] * 4 + [spec] * 4,
        out_specs=(spec,) * 4,
        scratch_shapes=scratch,
        compiler_params=pltpu.CompilerParams(
            collective_id=0, has_side_effects=True, vmem_limit_bytes=60 * 1024 * 1024
        ),
    )(
        state.reshape(L * rows, cols), cotangent.reshape(L * rows, cols), land_mask, level_count,
        fold_partner.reshape(1, cols), weight_in, weight_out.T, bias_hidden.reshape(1, H),
    )
    return out.reshape(L, rows, cols), g_in, g_out.T, g_bias.reshape(H)


def solution(mesh):
    placed = (
        P("ens", "lat", "lon"), P("ens", "lat", "lon"), P("lat", "lon"), P("lat", "lon"),
        P("lon"), P(), P(), P(),
    )
    body = functools.partial(on_device, mesh.shape["lat"], mesh.shape["lon"])
    return jax.shard_map(
        body,
        mesh=mesh,
        in_specs=placed,
        out_specs=(P("ens", "lat", "lon"), P("ens", None), P("ens", None), P("ens")),
        check_vma=False,
    )
```
